32 devices in a mesh: group: 2 (over x), gx: 8 (over z, y), gy: 2 (over core).
Axes of the slice: x: 2, y: 2, z: 4, core: 2. Of those that a mesh axis runs over, the one named last changes fastest.
Arguments:
- body_force: float32 [3, 32, 64, 512], P(None, ('group', 'gx'), 'gy'), parts along dimension 1, may hold values from -20 to 20
- phase_label: int32 [32, 64, 512], P(('group', 'gx'), 'gy'), parts along dimension 0, may hold values from 0 to 1
- grain_modulus: float32 [32, 64, 512], P(('group', 'gx'), 'gy'), parts along dimension 0, may hold values from 0.5 to 2
Outputs:
- displacement: float32 [3, 32, 64, 512], P(None, ('group', 'gx'), 'gy'), parts along dimension 1
- sensitivity: float32 [32, 64, 512], P(('group', 'gx'), 'gy'), parts along dimension 0
The draws below stay inside these ranges and needn't reach their ends.
There are 2 independent parts, one for each index of `group`. The reference program is written for one: setup_inputs(seed, part) draws one part's arguments, and reference() takes and returns one part's arrays. A program takes and returns all parts, laid end to end along the dimension named above; each array names one. Nothing has to cross between parts.
All inputs are finite; a program needn't handle non-finite values.
Results may differ from the reference program's by a relative error of at most 0.0002.
Values sent between devices are 32-bit elements; how exact they have to be, the bound alone decides.
A program may use at most 64 MiB of HBM per device.

```python
import math
import jax
import jax.numpy as jnp
import numpy as np
from jax import lax

ITERS = 3
NX = 16
NY = 64
NZ = 512


def smooth_load(key, amplitude):
    key_offsets, key_levels = jax.random.split(key, 2)
    offsets = jax.random.uniform(key_offsets, (3,), jnp.float32, 0.0, 1.0)
    levels = jax.random.uniform(key_levels, (3,), jnp.float32, 0.5, 1.0)
    x_share = jnp.arange(NX, dtype=jnp.float32) / NX
    y_share = jnp.arange(NY, dtype=jnp.float32) / NY
    z_share = (jnp.arange(NZ, dtype=jnp.float32) + 1.0) / NZ
    weight = amplitude * (0.5 - 0.5 * jnp.cos(2.0 * math.pi * (x_share + offsets[0])))
    across = jnp.cos(2.0 * math.pi * (x_share + offsets[1]))[:, None] * jnp.cos(2.0 * math.pi * (y_share + offsets[2]))[None, :]
    shape_xy = 1.0 + 0.5 * across
    profile = jnp.sin(0.5 * math.pi * z_share)
    return levels[:, None, None, None] * weight[None, :, None, None] * shape_xy[None, :, :, None] * profile[None, None, None, :]


def draw_body_force(key, part):
    key = jax.random.fold_in(key, 7)
    key_rough, key_smooth = jax.random.split(key, 2)
    position = jnp.arange(NX, dtype=jnp.float32) / (NX - 1)
    growth = (3.0 ** position)[None, :, None, None]
    random_part = jnp.clip(jax.random.normal(key_rough, (3, NX, NY, NZ), jnp.float32), -4.0, 4.0)
    values = random_part + smooth_load(key_smooth, 1.5)
    return values * growth


def draw_phase_label(key, part):
    key = jax.random.fold_in(key, 11)
    key_shift, key_cells = jax.random.split(key, 2)
    shift = jax.random.randint(key_shift, (), 0, NX, jnp.int32)
    plane = (jnp.arange(NX, dtype=jnp.int32) + shift) % NX
    distance = jnp.minimum(plane, NX - plane)
    pore_percent = 10 + 100 * distance // NX
    rolls = jax.random.randint(key_cells, (NX, NY, NZ), 0, 100, jnp.int32)
    return (rolls >= pore_percent[:, None, None]).astype(jnp.int32)


def steps_of(stream_key, shape, cuts, least, top_value):
    loudness = 1.0
    for dim, shards_of in cuts:
        draws = jax.random.uniform(jax.random.fold_in(jax.random.fold_in(stream_key, 6), dim), (shards_of,), jnp.float32, least / len(cuts), top_value / len(cuts))
        loudness = loudness * jnp.repeat(jnp.exp(draws), shape[dim] // shards_of).reshape((-1,) + (1,) * (len(shape) - 1 - dim))
    return loudness


def setup_inputs(seed: int = 0, part: int = 0) -> dict:
    keys = jax.random.split(jax.random.key(seed), 4)
    part_splits = jax.random.split(jax.random.fold_in(keys[3], part), 4)
    body_force = draw_body_force(jax.random.fold_in(jax.random.fold_in(keys[3], part), 71), part)
    phase_label = draw_phase_label(jax.random.fold_in(jax.random.fold_in(keys[3], part), 71), part)
    grain_modulus = jnp.clip(jnp.exp(math.log(2.0) - 1.3862944 * jax.random.uniform(part_splits[2], (NX, NY, NZ), jnp.float32) ** steps_of(part_splits[2], (NX, NY, NZ), ((0, 8), (1, 2)), -0.2, 0.2)), 0.5, 2.0)
    return {"body_force": body_force, "phase_label": phase_label, "grain_modulus": grain_modulus}


pore_modulus = 0.05

def element_matrix():
    poisson = 0.3
    lame = poisson / ((1.0 + poisson) * (1.0 - 2.0 * poisson))
    shear = 0.5 / (1.0 + poisson)
    elastic = np.zeros((6, 6))
    elastic[:3, :3] = lame
    for index in range(3):
        elastic[index, index] += 2.0 * shear
        elastic[index + 3, index + 3] = shear
    gauss = [0.5 - 0.5 / math.sqrt(3.0), 0.5 + 0.5 / math.sqrt(3.0)]
    matrix = np.zeros((24, 24))
    for point_x in gauss:
        for point_y in gauss:
            for point_z in gauss:
                strain = np.zeros((6, 24))
                corner = 0
                for side_x in (0, 1):
                    for side_y in (0, 1):
                        for side_z in (0, 1):
                            weight_x = point_x if side_x else 1.0 - point_x
                            weight_y = point_y if side_y else 1.0 - point_y
                            weight_z = point_z if side_z else 1.0 - point_z
                            slope_x = (2 * side_x - 1) * weight_y * weight_z
                            slope_y = (2 * side_y - 1) * weight_x * weight_z
                            slope_z = (2 * side_z - 1) * weight_x * weight_y
                            column = 3 * corner
                            strain[0, column] = slope_x
                            strain[1, column + 1] = slope_y
                            strain[2, column + 2] = slope_z
                            strain[3, column] = slope_y
                            strain[3, column + 1] = slope_x
                            strain[4, column + 1] = slope_z
                            strain[4, column + 2] = slope_y
                            strain[5, column] = slope_z
                            strain[5, column + 2] = slope_x
                            corner += 1
                matrix += strain.T @ elastic @ strain / 8.0
    return matrix.astype(np.float32)

def all_sides():
    return [(side_x, side_y, side_z) for side_x in (0, 1) for side_y in (0, 1) for side_z in (0, 1)]

def corner_view(extended, sides):
    view = extended[:, sides[0]:sides[0] + NX, sides[1]:sides[1] + NY]
    if sides[2] == 0:
        view = jnp.concatenate([jnp.zeros_like(view[..., :1]), view[..., :-1]], 3)
    return view

def place_force(summed, values, sides):
    if sides[2] == 0:
        values = jnp.concatenate([values[..., 1:], jnp.zeros_like(values[..., :1])], 3)
    return summed + jnp.pad(values, ((0, 0), (sides[0], 1 - sides[0]), (sides[1], 1 - sides[1]), (0, 0)))

def fold_periodic(summed):
    folded = summed[:, :NX].at[:, 0].add(summed[:, NX])
    return folded[:, :, :NY].at[:, :, 0].add(folded[:, :, NY])

def corner_forces(displacement, moduli, stiffness):
    extended = jnp.concatenate([displacement, displacement[:, :1]], 1)
    extended = jnp.concatenate([extended, extended[:, :, :1]], 2)
    views = [corner_view(extended, sides) for sides in all_sides()]
    forces = []
    for out_index in range(8):
        accum = jnp.zeros((3, NX, NY, NZ), jnp.float32)
        for in_index in range(8):
            block = stiffness[3 * out_index:3 * out_index + 3, 3 * in_index:3 * in_index + 3]
            accum = accum + jnp.einsum('pq,qxyz->pxyz', block, views[in_index], precision=lax.Precision.HIGHEST)
        forces.append(accum * moduli[None])
    return (views, forces)

def apply_operator(displacement, moduli, stiffness):
    views, forces = corner_forces(displacement, moduli, stiffness)
    summed = jnp.zeros((3, NX + 1, NY + 1, NZ), jnp.float32)
    for index, sides in enumerate(all_sides()):
        summed = place_force(summed, forces[index], sides)
    return fold_periodic(summed)

def reference(body_force, phase_label, grain_modulus):
    moduli = jnp.where(phase_label == 1, grain_modulus, jnp.float32(pore_modulus))
    stiffness = jnp.asarray(element_matrix(), dtype=jnp.float32)
    entries = jnp.diagonal(stiffness)
    summed = jnp.zeros((3, NX + 1, NY + 1, NZ), jnp.float32)
    for index, sides in enumerate(all_sides()):
        summed = place_force(summed, entries[3 * index:3 * index + 3][:, None, None, None] * moduli[None], sides)
    inverse = 1.0 / fold_periodic(summed)
    displacement = jnp.zeros_like(body_force)
    residual = body_force
    precond = inverse * residual
    direction = precond
    norm_now = jnp.sum(residual * precond)
    for step in range(ITERS):
        image = apply_operator(direction, moduli, stiffness)
        step_size = norm_now / jnp.sum(direction * image)
        displacement = displacement + step_size * direction
        residual = residual - step_size * image
        if step + 1 < ITERS:
            precond = inverse * residual
            norm_next = jnp.sum(residual * precond)
            direction = precond + norm_next / norm_now * direction
            norm_now = norm_next
    views, forces = corner_forces(displacement, moduli, stiffness)
    energy = jnp.zeros((NX, NY, NZ), jnp.float32)
    for index in range(8):
        energy = energy + lax.optimization_barrier(jnp.sum(views[index] * forces[index], axis=0))
    return (displacement, -energy)
```

```python
import functools
import math

import jax
import jax.numpy as jnp
import numpy as np
from jax import lax
from jax.experimental import pallas as pl
from jax.experimental.pallas import tpu as pltpu
from jax.sharding import PartitionSpec as P

PORE = 0.05
SHIFT = 1.0
MESH = pl.DeviceIdType.MESH


def element_matrix():
    poisson = 0.3
    lame = poisson / ((1.0 + poisson) * (1.0 - 2.0 * poisson))
    shear = 0.5 / (1.0 + poisson)
    elastic = np.zeros((6, 6))
    elastic[:3, :3] = lame
    for index in range(3):
        elastic[index, index] += 2.0 * shear
        elastic[index + 3, index + 3] = shear
    gauss = [0.5 - 0.5 / math.sqrt(3.0), 0.5 + 0.5 / math.sqrt(3.0)]
    matrix = np.zeros((24, 24))
    for px in gauss:
        for py in gauss:
            for pz in gauss:
                strain = np.zeros((6, 24))
                corner = 0
                for sx in (0, 1):
                    for sy in (0, 1):
                        for sz in (0, 1):
                            wx = px if sx else 1.0 - px
                            wy = py if sy else 1.0 - py
                            wz = pz if sz else 1.0 - pz
                            dx = (2 * sx - 1) * wy * wz
                            dy = (2 * sy - 1) * wx * wz
                            dz = (2 * sz - 1) * wx * wy
                            col = 3 * corner
                            strain[0, col] = dx
                            strain[1, col + 1] = dy
                            strain[2, col + 2] = dz
                            strain[3, col] = dy
                            strain[3, col + 1] = dx
                            strain[4, col + 1] = dz
                            strain[4, col + 2] = dy
                            strain[5, col] = dz
                            strain[5, col + 2] = dx
                            corner += 1
                matrix += strain.T @ elastic @ strain / 8.0
    return matrix


def mode_matrix():
    pair = np.array([[1.0, 1.0], [-1.0, 1.0]])
    full = np.kron(np.kron(np.kron(pair, pair), pair), np.eye(3))
    return full @ element_matrix() @ full.T / 64.0


K0_DIAGONAL = float(element_matrix()[0, 0])


def constants():
    k = mode_matrix()
    at = lambda mode, comp: 3 * mode + comp
    return dict(
        normal_own=k[at(4, 0), at(4, 0)] - k[at(4, 0), at(2, 1)],
        normal_all=k[at(4, 0), at(2, 1)],
        shear=k[at(2, 0), at(4, 1)],
        pair_own=k[at(6, 0), at(6, 0)],
        pair_other=k[at(6, 0), at(3, 2)],
        triple=k[at(3, 0), at(5, 1)],
        third=k[at(7, 0), at(7, 0)],
    )


K = {name: float(value) for name, value in constants().items()}


def mode_forces(m, modulus):
    g = {}
    own, every = modulus * K["normal_own"], modulus * K["normal_all"]
    keys = [(4, 0), (2, 1), (1, 2)]
    total = every * (m[keys[0]] + m[keys[1]] + m[keys[2]])
    for key in keys:
        g[key] = own * m[key] + total
    shear = modulus * K["shear"]
    for first, second in (((2, 0), (4, 1)), ((1, 1), (2, 2)), ((1, 0), (4, 2))):
        g[first] = g[second] = shear * (m[first] + m[second])
    own, other = modulus * K["pair_own"], modulus * K["pair_other"]
    for first, second in (((6, 0), (3, 2)), ((6, 1), (5, 2)), ((5, 0), (3, 1))):
        g[first] = own * m[first] + other * m[second]
        g[second] = own * m[second] + other * m[first]
    keys = [(3, 0), (5, 1), (6, 2)]
    triple = modulus * K["triple"]
    total = m[keys[0]] + m[keys[1]] + m[keys[2]]
    for key in keys:
        g[key] = triple * (m[key] + total)
    third = modulus * K["third"]
    for comp in range(3):
        g[(7, comp)] = third * m[(7, comp)]
    return g


def mode_energy(m):
    a, b, c = m[(4, 0)], m[(2, 1)], m[(1, 2)]
    total = a + b + c
    energy = K["normal_own"] * (a * a + b * b + c * c) + K["normal_all"] * (total * total)
    squares = None
    for first, second in (((2, 0), (4, 1)), ((1, 1), (2, 2)), ((1, 0), (4, 2))):
        both = m[first] + m[second]
        squares = both * both if squares is None else squares + both * both
    energy = energy + K["shear"] * squares
    squares = cross = None
    for first, second in (((6, 0), (3, 2)), ((6, 1), (5, 2)), ((5, 0), (3, 1))):
        square = m[first] * m[first] + m[second] * m[second]
        product = m[first] * m[second]
        squares = square if squares is None else squares + square
        cross = product if cross is None else cross + product
    energy = energy + K["pair_own"] * squares + (2.0 * K["pair_other"]) * cross
    a, b, c = m[(3, 0)], m[(5, 1)], m[(6, 2)]
    total = a + b + c
    energy = energy + K["triple"] * (a * a + b * b + c * c + total * total)
    a, b, c = m[(7, 0)], m[(7, 1)], m[(7, 2)]
    return energy + K["third"] * (a * a + b * b + c * c)


def kernel(
    n_gx, xc, yc, zc,
    force, label, grain, disp_out, sens_out,
    u0, u1, u2, edge_out, edge_in, mod_own, mod_halo, mod_edge_out, mod_edge_in,
    mod_ext, diag, inv, yz, out, sums, tile, tiles, send_sem, recv_sem, tile_send, tile_recv,
):
    levels = [u0, u1, u2]
    rows = yc + 8
    base = 8
    gx, gy = lax.axis_index("gx"), lax.axis_index("gy")
    other = 1 - gy
    nxt, prv = lax.rem(gx + 1, n_gx), lax.rem(gx + n_gx - 1, n_gx)
    peers = []
    for step in range(n_gx):
        for flip in (0, 1):
            if step or flip:
                peers.append({
                    "gx": lax.rem(gx + step, n_gx) if step else gx,
                    "gy": other if flip else gy,
                })

    barrier = pltpu.get_barrier_semaphore()
    for peer in peers:
        pl.semaphore_signal(barrier, inc=1, device_id=peer, device_id_type=MESH)

    lane = lax.broadcasted_iota(jnp.int32, (1, zc), 1)

    def below(value):
        return jnp.where(lane == 0, 0.0, pltpu.roll(value, 1, 1))

    def above(value):
        return jnp.where(lane == zc - 1, 0.0, pltpu.roll(value, zc - 1, 1))

    sent = []

    def send(src, dst, to_gx, to_gy):
        copy = pltpu.make_async_remote_copy(
            src_ref=src, dst_ref=dst,
            send_sem=send_sem.at[len(sent)], recv_sem=recv_sem.at[len(sent)],
            device_id={"gx": to_gx, "gy": to_gy}, device_id_type=MESH,
        )
        copy.start()
        sent.append(copy)
        return copy

    for x in range(xc):
        values = jnp.where(label[x] == 1, grain[x], jnp.float32(PORE))
        mod_own[x] = values
        mod_edge_out[x, 0:1] = values[yc - 1 : yc]
        mod_ext[x + 1, 1 : yc + 1] = values
    for x in range(xc + 1):
        mod_ext[x, yc + 1 : rows] = jnp.zeros((rows - yc - 1, zc), jnp.float32)
    for u in levels:
        for c in range(3):
            for x in range(xc + 2):
                u[c, x, base + yc : base + yc + 8] = jnp.zeros((8, zc), jnp.float32)
    for x in range(xc):
        mod_edge_out[x, 1:8] = jnp.zeros((7, zc), jnp.float32)
        for level in range(3):
            edge_out[level, x, 6:8] = jnp.zeros((2, zc), jnp.float32)
    sums[...] = jnp.zeros_like(sums)

    pl.semaphore_wait(barrier, len(peers))
    mod_y = send(mod_edge_out, mod_edge_in.at[pl.ds(1, xc)], gx, other)
    mod_x = send(mod_own.at[xc - 1], mod_halo, nxt, gy)
    mod_xy = send(mod_edge_out.at[xc - 1], mod_edge_in.at[0], nxt, other)

    def folded(value):
        total = None
        for r in range(value.shape[0] // 8):
            for l in range(zc // 128):
                part = value[8 * r : 8 * r + 8, 128 * l : 128 * l + 128]
                total = part if total is None else total + part
        return total

    def set_edges(level, x, c, value):
        edge_out[level, x - 1, c : c + 1] = value[0:1]
        edge_out[level, x - 1, 3 + c : 4 + c] = value[yc - 1 : yc]

    own = pl.ds(base, yc)

    def send_y(level):
        return send(edge_out.at[level], edge_in.at[level, pl.ds(1, xc)], gx, other)

    def send_next(level):
        u = levels[level]
        return (
            send(u.at[:, xc, own], u.at[:, 0, own], nxt, gy),
            send(edge_out.at[level, xc - 1], edge_in.at[level, 0], nxt, other),
        )

    def send_prev(level):
        u = levels[level]
        return (
            send(u.at[:, 1, own], u.at[:, xc + 1, own], prv, gy),
            send(edge_out.at[level, 0], edge_in.at[level, xc + 1], prv, other),
        )

    def fill_edges(level, x):
        for c in range(3):
            levels[level][c, x, base + yc : base + yc + 1] = edge_in[level, x, c : c + 1]
            levels[level][c, x, base - 1 : base] = edge_in[level, x, 3 + c : 4 + c]

    def start_plane(x):
        total = mod_ext[x - 1, 0:yc] + mod_ext[x - 1, 1 : yc + 1]
        total = total + mod_ext[x, 0:yc] + mod_ext[x, 1 : yc + 1]
        total = (total + above(total)) * K0_DIAGONAL
        inverse = 1.0 / total
        diag[x - 1] = total
        inv[x - 1] = inverse
        for c in range(3):
            load = force[c, x - 1]
            value = inverse * load
            u0[c, x, base : base + yc] = value
            set_edges(0, x, c, value)
            sums[0] += folded(value * load)

    mod_y.wait_recv()
    for x in range(1, xc + 1):
        mod_ext[x, 0:1] = mod_edge_in[x, 0:1]
    for x in range(xc, 1, -1):
        start_plane(x)
    from_prev = send_next(0)
    mod_x.wait_recv()
    mod_xy.wait_recv()
    mod_ext[0, 0:1] = mod_edge_in[0, 0:1]
    mod_ext[0, 1 : yc + 1] = mod_halo[...]
    start_plane(1)
    from_next = send_prev(0)
    from_y = send_y(0)

    def split_modes(u, x, first, count):
        for c in range(3):
            low = u[c, x, base + first : base + first + count]
            high = u[c, x, base + first + 1 : base + first + 1 + count]
            total, change = high + low, high - low
            low = below(total)
            yz[0, c, x, 0:count] = total + low
            yz[1, c, x, 0:count] = total - low
            low = below(change)
            yz[2, c, x, 0:count] = change + low
            yz[3, c, x, 0:count] = change - low

    def modes_of(cell, r, l):
        m = {}
        for q in range(4):
            for c in range(3):
                low, high = yz[q, c, cell, r, l], yz[q, c, cell + 1, r, l]
                if q:
                    m[(q, c)] = high + low
                m[(4 + q, c)] = high - low
        return m

    lanes = zc // 128

    def apply_cell(cell):
        def body(t, carry):
            r = pl.ds(pl.multiple_of(t // lanes * 8, 8), 8)
            l = pl.ds(pl.multiple_of(lax.rem(t, lanes) * 128, 128), 128)
            g = mode_forces(modes_of(cell, r, l), mod_ext[cell, r, l])
            for q in range(4):
                for c in range(3):
                    if cell >= 1:
                        value = g[(q, c)] - g[(4 + q, c)] if q else -g[(4 + q, c)]
                        if cell == xc:
                            value = value + out[q, c, cell - 1, r, l] if xc > 1 else value
                        elif cell > 1:
                            value = value + out[q, c, cell - 1, r, l]
                        out[q, c, cell - 1, r, l] = value
                    if cell + 1 <= xc:
                        value = g[(q, c)] + g[(4 + q, c)] if q else g[(4 + q, c)]
                        if cell == 0:
                            value = value + out[q, c, cell, r, l]
                        out[q, c, cell, r, l] = value
            return carry

        lax.fori_loop(0, rows // 8 * lanes, body, 0)

    def next_plane(level, x):
        u, v = levels[level], levels[level + 1]
        for c in range(3):
            part = lambda q, start: out[q, c, x - 1, start : start + yc]
            even = (part(0, 0) + part(2, 0)) + (part(0, 1) - part(2, 1))
            odd = (part(1, 0) + part(3, 0)) + (part(1, 1) - part(3, 1))
            image = (even + odd) + above(even - odd)
            value = u[c, x, base : base + yc]
            weighted = image - SHIFT * (diag[x - 1] * value)
            following = inv[x - 1] * weighted
            v[c, x, base : base + yc] = following
            set_edges(level + 1, x, c, following)
            sums[2 * level + 1] += folded(value * weighted)
            sums[2 * level + 2] += folded(following * weighted)

    for level in range(2):
        u = levels[level]
        from_y.wait_recv()
        for x in range(1, xc + 1):
            fill_edges(level, x)
            split_modes(u, x, -1, rows)
        for cell in range(1, xc):
            apply_cell(cell)
        for copy in from_next:
            copy.wait_recv()
        fill_edges(level, xc + 1)
        split_modes(u, xc + 1, -1, rows)
        apply_cell(xc)
        for x in range(xc, 1, -1):
            next_plane(level, x)
        if level == 0:
            later_prev = send_next(1)
        for copy in from_prev:
            copy.wait_recv()
        fill_edges(level, 0)
        split_modes(u, 0, -1, rows)
        apply_cell(0)
        next_plane(level, 1)
        from_next = send_prev(level + 1)
        from_y = send_y(level + 1)
        if level == 0:
            from_prev = later_prev

    def energies(cell, put):
        def body(t, carry):
            r = pl.ds(pl.multiple_of(t // lanes * 8, 8), 8)
            l = pl.ds(pl.multiple_of(lax.rem(t, lanes) * 128, 128), 128)
            put(r, l, mod_own[cell - 1, r, l] * mode_energy(modes_of(cell, r, l)))
            return carry

        lax.fori_loop(0, yc // 8 * lanes, body, 0)

    def add_energy(r, l, value):
        sums[5] += value

    from_y.wait_recv()
    for x in range(1, xc + 1):
        fill_edges(2, x)
        split_modes(u2, x, 0, yc)
    for cell in range(1, xc):
        energies(cell, add_energy)
    for copy in from_next:
        copy.wait_recv()
    fill_edges(2, xc + 1)
    split_modes(u2, xc + 1, 0, yc)
    energies(xc, add_energy)

    tile[...] = jnp.sum(sums[...], axis=1)
    copies = []
    for index, peer in enumerate(peers):
        copy = pltpu.make_async_remote_copy(
            src_ref=tile, dst_ref=tiles.at[index],
            send_sem=tile_send.at[index], recv_sem=tile_recv.at[index],
            device_id=peer, device_id_type=MESH,
        )
        copy.start()
        copies.append(copy)
    total = tile[...]
    for index, copy in enumerate(copies):
        copy.wait_recv()
        total = total + tiles[index]
    total = jnp.sum(total, axis=1, keepdims=True)
    h = [total[k : k + 1] for k in range(6)]
    h[5] = h[5] - SHIFT * h[4]

    def inner(first, second, shifted):
        result = None
        for i, a in enumerate(first):
            for j, b in enumerate(second):
                moment = h[i + j + 1] + SHIFT * h[i + j] if shifted else h[i + j]
                term = a * b * moment
                result = term if result is None else result + term
        return result

    one = jnp.ones_like(h[0])
    precond, direction = [one], [one]
    weights = [jnp.zeros_like(one)] * 3
    norm_now = h[0]
    for step in range(3):
        alpha = norm_now / inner(direction, direction, True)
        for i, d in enumerate(direction):
            weights[i] = weights[i] + alpha * d
        if step < 2:
            image = [SHIFT * d for d in direction] + [jnp.zeros_like(one)]
            for i, d in enumerate(direction):
                image[i + 1] = image[i + 1] + d
            precond = precond + [jnp.zeros_like(one)] * (len(image) - len(precond))
            precond = [p - alpha * q for p, q in zip(precond, image)]
            norm_next = inner(precond, precond, False)
            beta = norm_next / norm_now
            longer = direction + [jnp.zeros_like(one)]
            direction = [p + beta * d for p, d in zip(precond, longer)]
            norm_now = norm_next

    for copy in sent:
        copy.wait_send()
    for copy in copies:
        copy.wait_send()
    for x in range(1, xc + 2):
        for c in range(3):
            where = (c, x, slice(base, base + yc + 8))
            value = weights[0] * u0[where] + weights[1] * u1[where] + weights[2] * u2[where]
            u0[where] = value
            if x <= xc:
                disp_out[c, x - 1] = value[0:yc]
        split_modes(u0, x, 0, yc)

    for cell in range(1, xc + 1):
        def put(r, l, value, cell=cell):
            sens_out[cell - 1, r, l] = -value

        energies(cell, put)


def per_device(n_gx, body_force, phase_label, grain_modulus):
    xc, yc, zc = phase_label.shape
    peers = 2 * n_gx - 1
    f32 = jnp.float32
    vmem = pltpu.VMEM
    ext = vmem((3, xc + 2, yc + 16, zc), f32)
    return pl.pallas_call(
        functools.partial(kernel, n_gx, xc, yc, zc),
        out_shape=(
            jax.ShapeDtypeStruct(body_force.shape, f32),
            jax.ShapeDtypeStruct(phase_label.shape, f32),
        ),
        in_specs=[pl.BlockSpec(memory_space=pltpu.VMEM)] * 3,
        out_specs=(pl.BlockSpec(memory_space=pltpu.VMEM),) * 2,
        scratch_shapes=[
            ext, ext, ext,
            vmem((3, xc, 8, zc), f32),
            vmem((3, xc + 2, 8, zc), f32),
            vmem((xc, yc, zc), f32),
            vmem((yc, zc), f32),
            vmem((xc, 8, zc), f32),
            vmem((xc + 1, 8, zc), f32),
            vmem((xc + 1, yc + 8, zc), f32),
            vmem((xc, yc, zc), f32),
            vmem((xc, yc, zc), f32),
            vmem((4, 3, xc + 2, yc + 8, zc), f32),
            vmem((4, 3, xc, yc + 8, zc), f32),
            vmem((8, 8, 128), f32),
            vmem((8, 128), f32),
            vmem((peers, 8, 128), f32),
            pltpu.SemaphoreType.DMA((16,)),
            pltpu.SemaphoreType.DMA((16,)),
            pltpu.SemaphoreType.DMA((peers,)),
            pltpu.SemaphoreType.DMA((peers,)),
        ],
        compiler_params=pltpu.CompilerParams(
            collective_id=0, has_side_effects=True, vmem_limit_bytes=40 * 1024 * 1024
        ),
        cost_estimate=pl.CostEstimate(
            flops=600 * xc * yc * zc, bytes_accessed=40 * xc * yc * zc, transcendentals=0
        ),
    )(body_force, phase_label, grain_modulus)


def solution(mesh):
    in_specs = (
        P(None, ("group", "gx"), "gy", None),
        P(("group", "gx"), "gy", None),
        P(("group", "gx"), "gy", None),
    )
    out_specs = (P(None, ("group", "gx"), "gy", None), P(("group", "gx"), "gy", None))
    return jax.shard_map(
        functools.partial(per_device, mesh.shape["gx"]),
        mesh=mesh, in_specs=in_specs, out_specs=out_specs, check_vma=False,
    )
```

```python
import functools
import math

import jax
import jax.numpy as jnp
import numpy as np
from jax import lax
from jax.experimental import pallas as pl
from jax.experimental.pallas import tpu as pltpu
from jax.sharding import PartitionSpec as P

PORE = 0.05
SHIFT = 1.0
MESH = pl.DeviceIdType.MESH


def element_matrix():
    poisson = 0.3
    lame = poisson / ((1.0 + poisson) * (1.0 - 2.0 * poisson))
    shear = 0.5 / (1.0 + poisson)
    elastic = np.zeros((6, 6))
    elastic[:3, :3] = lame
    for index in range(3):
        elastic[index, index] += 2.0 * shear
        elastic[index + 3, index + 3] = shear
    gauss = [0.5 - 0.5 / math.sqrt(3.0), 0.5 + 0.5 / math.sqrt(3.0)]
    matrix = np.zeros((24, 24))
    for px in gauss:
        for py in gauss:
            for pz in gauss:
                strain = np.zeros((6, 24))
                corner = 0
                for sx in (0, 1):
                    for sy in (0, 1):
                        for sz in (0, 1):
                            wx = px if sx else 1.0 - px
                            wy = py if sy else 1.0 - py
                            wz = pz if sz else 1.0 - pz
                            dx = (2 * sx - 1) * wy * wz
                            dy = (2 * sy - 1) * wx * wz
                            dz = (2 * sz - 1) * wx * wy
                            col = 3 * corner
                            strain[0, col] = dx
                            strain[1, col + 1] = dy
                            strain[2, col + 2] = dz
                            strain[3, col] = dy
                            strain[3, col + 1] = dx
                            strain[4, col + 1] = dz
                            strain[4, col + 2] = dy
                            strain[5, col] = dz
                            strain[5, col + 2] = dx
                            corner += 1
                matrix += strain.T @ elastic @ strain / 8.0
    return matrix


def mode_matrix():
    pair = np.array([[1.0, 1.0], [-1.0, 1.0]])
    full = np.kron(np.kron(np.kron(pair, pair), pair), np.eye(3))
    return full @ element_matrix() @ full.T / 64.0


K0_DIAGONAL = float(element_matrix()[0, 0])


def constants():
    k = mode_matrix()
    at = lambda mode, comp: 3 * mode + comp
    return dict(
        normal_own=k[at(4, 0), at(4, 0)] - k[at(4, 0), at(2, 1)],
        normal_all=k[at(4, 0), at(2, 1)],
        shear=k[at(2, 0), at(4, 1)],
        pair_own=k[at(6, 0), at(6, 0)],
        pair_other=k[at(6, 0), at(3, 2)],
        triple=k[at(3, 0), at(5, 1)],
        third=k[at(7, 0), at(7, 0)],
    )


K = {name: float(value) for name, value in constants().items()}


def mode_forces(m, modulus):
    g = {}
    own, every = modulus * K["normal_own"], modulus * K["normal_all"]
    keys = [(4, 0), (2, 1), (1, 2)]
    total = every * (m[keys[0]] + m[keys[1]] + m[keys[2]])
    for key in keys:
        g[key] = own * m[key] + total
    shear = modulus * K["shear"]
    for first, second in (((2, 0), (4, 1)), ((1, 1), (2, 2)), ((1, 0), (4, 2))):
        g[first] = g[second] = shear * (m[first] + m[second])
    own, other = modulus * K["pair_own"], modulus * K["pair_other"]
    for first, second in (((6, 0), (3, 2)), ((6, 1), (5, 2)), ((5, 0), (3, 1))):
        g[first] = own * m[first] + other * m[second]
        g[second] = own * m[second] + other * m[first]
    keys = [(3, 0), (5, 1), (6, 2)]
    triple = modulus * K["triple"]
    total = m[keys[0]] + m[keys[1]] + m[keys[2]]
    for key in keys:
        g[key] = triple * (m[key] + total)
    third = modulus * K["third"]
    for comp in range(3):
        g[(7, comp)] = third * m[(7, comp)]
    return g


def mode_energy(m):
    a, b, c = m[(4, 0)], m[(2, 1)], m[(1, 2)]
    total = a + b + c
    energy = K["normal_own"] * (a * a + b * b + c * c) + K["normal_all"] * (total * total)
    squares = None
    for first, second in (((2, 0), (4, 1)), ((1, 1), (2, 2)), ((1, 0), (4, 2))):
        both = m[first] + m[second]
        squares = both * both if squares is None else squares + both * both
    energy = energy + K["shear"] * squares
    squares = cross = None
    for first, second in (((6, 0), (3, 2)), ((6, 1), (5, 2)), ((5, 0), (3, 1))):
        square = m[first] * m[first] + m[second] * m[second]
        product = m[first] * m[second]
        squares = square if squares is None else squares + square
        cross = product if cross is None else cross + product
    energy = energy + K["pair_own"] * squares + (2.0 * K["pair_other"]) * cross
    a, b, c = m[(3, 0)], m[(5, 1)], m[(6, 2)]
    total = a + b + c
    energy = energy + K["triple"] * (a * a + b * b + c * c + total * total)
    a, b, c = m[(7, 0)], m[(7, 1)], m[(7, 2)]
    return energy + K["third"] * (a * a + b * b + c * c)


def kernel(
    n_gx, xc, yc, zc,
    force_in, label_in, grain_in, disp_out, sens_out,
    force, label, grain, in_sem,
    u0, u1, u2, edge_out, edge_in, mod_own, mod_halo, mod_edge_out, mod_edge_in,
    mod_ext, diag, inv, yz, out, sums, tile, tiles, send_sem, recv_sem, tile_send, tile_recv,
):
    levels = [u0, u1, u2]
    rows = yc + 8
    base = 8
    gx, gy = lax.axis_index("gx"), lax.axis_index("gy")
    other = 1 - gy
    nxt, prv = lax.rem(gx + 1, n_gx), lax.rem(gx + n_gx - 1, n_gx)
    peers = []
    for step in range(n_gx):
        for flip in (0, 1):
            if step or flip:
                peers.append({
                    "gx": lax.rem(gx + step, n_gx) if step else gx,
                    "gy": other if flip else gy,
                })

    loads = []
    for index, (src, dst) in enumerate(((label_in, label), (grain_in, grain), (force_in, force))):
        load = pltpu.make_async_copy(src, dst, in_sem.at[index])
        load.start()
        loads.append(load)
    barrier = pltpu.get_barrier_semaphore()
    for peer in peers:
        pl.semaphore_signal(barrier, inc=1, device_id=peer, device_id_type=MESH)

    lane = lax.broadcasted_iota(jnp.int32, (1, zc), 1)

    def below(value):
        return jnp.where(lane == 0, 0.0, pltpu.roll(value, 1, 1))

    def above(value):
        return jnp.where(lane == zc - 1, 0.0, pltpu.roll(value, zc - 1, 1))

    sent = []

    def send(src, dst, to_gx, to_gy):
        copy = pltpu.make_async_remote_copy(
            src_ref=src, dst_ref=dst,
            send_sem=send_sem.at[len(sent)], recv_sem=recv_sem.at[len(sent)],
            device_id={"gx": to_gx, "gy": to_gy}, device_id_type=MESH,
        )
        copy.start()
        sent.append(copy)
        return copy

    for x in range(xc + 1):
        mod_ext[x, yc + 1 : rows] = jnp.zeros((rows - yc - 1, zc), jnp.float32)
    for u in levels:
        for c in range(3):
            for x in range(xc + 2):
                u[c, x, base + yc : base + yc + 8] = jnp.zeros((8, zc), jnp.float32)
    for x in range(xc):
        mod_edge_out[x, 1:8] = jnp.zeros((7, zc), jnp.float32)
        for level in range(3):
            edge_out[level, x, 6:8] = jnp.zeros((2, zc), jnp.float32)
    sums[...] = jnp.zeros_like(sums)

    loads[0].wait()
    loads[1].wait()
    for x in range(xc):
        values = jnp.where(label[x] == 1, grain[x], jnp.float32(PORE))
        mod_own[x] = values
        mod_edge_out[x, 0:1] = values[yc - 1 : yc]
        mod_ext[x + 1, 1 : yc + 1] = values
    pl.semaphore_wait(barrier, len(peers))
    mod_y = send(mod_edge_out, mod_edge_in.at[pl.ds(1, xc)], gx, other)
    mod_x = send(mod_own.at[xc - 1], mod_halo, nxt, gy)
    mod_xy = send(mod_edge_out.at[xc - 1], mod_edge_in.at[0], nxt, other)

    def folded(value):
        total = None
        for r in range(value.shape[0] // 8):
            for l in range(zc // 128):
                part = value[8 * r : 8 * r + 8, 128 * l : 128 * l + 128]
                total = part if total is None else total + part
        return total

    def set_edges(level, x, c, value):
        edge_out[level, x - 1, c : c + 1] = value[0:1]
        edge_out[level, x - 1, 3 + c : 4 + c] = value[yc - 1 : yc]

    own = pl.ds(base, yc)

    def send_y(level):
        return send(edge_out.at[level], edge_in.at[level, pl.ds(1, xc)], gx, other)

    def face_next(level, c):
        u = levels[level]
        return send(u.at[c, xc, own], u.at[c, 0, own], nxt, gy)

    def face_prev(level, c):
        u = levels[level]
        return send(u.at[c, 1, own], u.at[c, xc + 1, own], prv, gy)

    def rows_next(level):
        return send(edge_out.at[level, xc - 1], edge_in.at[level, 0], nxt, other)

    def rows_prev(level):
        return send(edge_out.at[level, 0], edge_in.at[level, xc + 1], prv, other)

    def fill_edges(level, x):
        for c in range(3):
            levels[level][c, x, base + yc : base + yc + 1] = edge_in[level, x, c : c + 1]
            levels[level][c, x, base - 1 : base] = edge_in[level, x, 3 + c : 4 + c]

    from_prev, from_next = [[], [], []], [[], [], []]

    def faces(x, level, c):
        if x == xc and level < 2:
            from_prev[level].append(face_next(level, c))
        if x == 1:
            from_next[level].append(face_prev(level, c))

    def start_plane(x, faces):
        total = mod_ext[x - 1, 0:yc] + mod_ext[x - 1, 1 : yc + 1]
        total = total + mod_ext[x, 0:yc] + mod_ext[x, 1 : yc + 1]
        total = (total + above(total)) * K0_DIAGONAL
        inverse = 1.0 / total
        diag[x - 1] = total
        inv[x - 1] = inverse
        for c in range(3):
            load = force[c, x - 1]
            value = inverse * load
            u0[c, x, base : base + yc] = value
            set_edges(0, x, c, value)
            faces(x, 0, c)
            sums[0] += folded(value * load)

    loads[2].wait()
    mod_y.wait_recv()
    for x in range(1, xc + 1):
        mod_ext[x, 0:1] = mod_edge_in[x, 0:1]
    for x in range(xc, 1, -1):
        start_plane(x, faces)
        if x == xc:
            from_prev[0].append(rows_next(0))
    mod_x.wait_recv()
    mod_xy.wait_recv()
    mod_ext[0, 0:1] = mod_edge_in[0, 0:1]
    mod_ext[0, 1 : yc + 1] = mod_halo[...]
    start_plane(1, faces)
    if xc == 1:
        from_prev[0].append(rows_next(0))
    from_next[0].append(rows_prev(0))
    from_y = send_y(0)

    def split_modes(u, x, first, count):
        for c in range(3):
            low = u[c, x, base + first : base + first + count]
            high = u[c, x, base + first + 1 : base + first + 1 + count]
            total, change = high + low, high - low
            low = below(total)
            yz[0, c, x, 0:count] = total + low
            yz[1, c, x, 0:count] = total - low
            low = below(change)
            yz[2, c, x, 0:count] = change + low
            yz[3, c, x, 0:count] = change - low

    def modes_of(cell, r, l):
        m = {}
        for q in range(4):
            for c in range(3):
                low, high = yz[q, c, cell, r, l], yz[q, c, cell + 1, r, l]
                if q:
                    m[(q, c)] = high + low
                m[(4 + q, c)] = high - low
        return m

    lanes = zc // 128

    def apply_cell(cell):
        def body(t, carry):
            r = pl.ds(pl.multiple_of(t // lanes * 8, 8), 8)
            l = pl.ds(pl.multiple_of(lax.rem(t, lanes) * 128, 128), 128)
            g = mode_forces(modes_of(cell, r, l), mod_ext[cell, r, l])
            for q in range(4):
                for c in range(3):
                    if cell >= 1:
                        value = g[(q, c)] - g[(4 + q, c)] if q else -g[(4 + q, c)]
                        if cell == xc:
                            value = value + out[q, c, cell - 1, r, l] if xc > 1 else value
                        elif cell > 1:
                            value = value + out[q, c, cell - 1, r, l]
                        out[q, c, cell - 1, r, l] = value
                    if cell + 1 <= xc:
                        value = g[(q, c)] + g[(4 + q, c)] if q else g[(4 + q, c)]
                        if cell == 0:
                            value = value + out[q, c, cell, r, l]
                        out[q, c, cell, r, l] = value
            return carry

        lax.fori_loop(0, rows // 8 * lanes, body, 0)

    def next_plane(level, x):
        u, v = levels[level], levels[level + 1]
        for c in range(3):
            part = lambda q, start: out[q, c, x - 1, start : start + yc]
            even = (part(0, 0) + part(2, 0)) + (part(0, 1) - part(2, 1))
            odd = (part(1, 0) + part(3, 0)) + (part(1, 1) - part(3, 1))
            image = (even + odd) + above(even - odd)
            value = u[c, x, base : base + yc]
            weighted = image - SHIFT * (diag[x - 1] * value)
            following = inv[x - 1] * weighted
            v[c, x, base : base + yc] = following
            set_edges(level + 1, x, c, following)
            faces(x, level + 1, c)
            sums[2 * level + 1] += folded(value * weighted)
            sums[2 * level + 2] += folded(following * weighted)

    for level in range(2):
        u = levels[level]
        from_y.wait_recv()
        for x in range(1, xc + 1):
            fill_edges(level, x)
            split_modes(u, x, -1, rows)
        for cell in range(1, xc):
            apply_cell(cell)
        for copy in from_next[level]:
            copy.wait_recv()
        fill_edges(level, xc + 1)
        split_modes(u, xc + 1, -1, rows)
        apply_cell(xc)
        for x in range(xc, 1, -1):
            next_plane(level, x)
            if x == xc and level == 0:
                from_prev[1].append(rows_next(1))
        for copy in from_prev[level]:
            copy.wait_recv()
        fill_edges(level, 0)
        split_modes(u, 0, -1, rows)
        apply_cell(0)
        next_plane(level, 1)
        if xc == 1 and level == 0:
            from_prev[1].append(rows_next(1))
        from_next[level + 1].append(rows_prev(level + 1))
        from_y = send_y(level + 1)

    def energies(cell, put):
        def body(t, carry):
            r = pl.ds(pl.multiple_of(t // lanes * 8, 8), 8)
            l = pl.ds(pl.multiple_of(lax.rem(t, lanes) * 128, 128), 128)
            put(r, l, mod_own[cell - 1, r, l] * mode_energy(modes_of(cell, r, l)))
            return carry

        lax.fori_loop(0, yc // 8 * lanes, body, 0)

    def add_energy(r, l, value):
        sums[5] += value

    from_y.wait_recv()
    for x in range(1, xc + 1):
        fill_edges(2, x)
        split_modes(u2, x, 0, yc)
    for cell in range(1, xc):
        energies(cell, add_energy)
    for copy in from_next[2]:
        copy.wait_recv()
    fill_edges(2, xc + 1)
    split_modes(u2, xc + 1, 0, yc)
    energies(xc, add_energy)

    tile[...] = jnp.sum(sums[...], axis=1)
    copies = []
    for index, peer in enumerate(peers):
        copy = pltpu.make_async_remote_copy(
            src_ref=tile, dst_ref=tiles.at[index],
            send_sem=tile_send.at[index], recv_sem=tile_recv.at[index],
            device_id=peer, device_id_type=MESH,
        )
        copy.start()
        copies.append(copy)
    total = tile[...]
    for index, copy in enumerate(copies):
        copy.wait_recv()
        total = total + tiles[index]
    total = jnp.sum(total, axis=1, keepdims=True)
    h = [total[k : k + 1] for k in range(6)]
    h[5] = h[5] - SHIFT * h[4]

    def inner(first, second, shifted):
        result = None
        for i, a in enumerate(first):
            for j, b in enumerate(second):
                moment = h[i + j + 1] + SHIFT * h[i + j] if shifted else h[i + j]
                term = a * b * moment
                result = term if result is None else result + term
        return result

    one = jnp.ones_like(h[0])
    precond, direction = [one], [one]
    weights = [jnp.zeros_like(one)] * 3
    norm_now = h[0]
    for step in range(3):
        alpha = norm_now / inner(direction, direction, True)
        for i, d in enumerate(direction):
            weights[i] = weights[i] + alpha * d
        if step < 2:
            image = [SHIFT * d for d in direction] + [jnp.zeros_like(one)]
            for i, d in enumerate(direction):
                image[i + 1] = image[i + 1] + d
            precond = precond + [jnp.zeros_like(one)] * (len(image) - len(precond))
            precond = [p - alpha * q for p, q in zip(precond, image)]
            norm_next = inner(precond, precond, False)
            beta = norm_next / norm_now
            longer = direction + [jnp.zeros_like(one)]
            direction = [p + beta * d for p, d in zip(precond, longer)]
            norm_now = norm_next

    for copy in sent:
        copy.wait_send()
    for copy in copies:
        copy.wait_send()
    for x in range(1, xc + 2):
        for c in range(3):
            where = (c, x, slice(base, base + yc + 8))
            value = weights[0] * u0[where] + weights[1] * u1[where] + weights[2] * u2[where]
            u0[where] = value
            if x <= xc:
                disp_out[c, x - 1] = value[0:yc]
        split_modes(u0, x, 0, yc)

    for cell in range(1, xc + 1):
        def put(r, l, value, cell=cell):
            sens_out[cell - 1, r, l] = -value

        energies(cell, put)


def per_device(n_gx, body_force, phase_label, grain_modulus):
    xc, yc, zc = phase_label.shape
    peers = 2 * n_gx - 1
    f32 = jnp.float32
    vmem = pltpu.VMEM
    ext = vmem((3, xc + 2, yc + 16, zc), f32)
    return pl.pallas_call(
        functools.partial(kernel, n_gx, xc, yc, zc),
        out_shape=(
            jax.ShapeDtypeStruct(body_force.shape, f32),
            jax.ShapeDtypeStruct(phase_label.shape, f32),
        ),
        in_specs=[pl.BlockSpec(memory_space=pl.ANY)] * 3,
        out_specs=(pl.BlockSpec(memory_space=pltpu.VMEM),) * 2,
        scratch_shapes=[
            vmem((3, xc, yc, zc), f32),
            vmem((xc, yc, zc), jnp.int32),
            vmem((xc, yc, zc), f32),
            pltpu.SemaphoreType.DMA((3,)),
            ext, ext, ext,
            vmem((3, xc, 8, zc), f32),
            vmem((3, xc + 2, 8, zc), f32),
            vmem((xc, yc, zc), f32),
            vmem((yc, zc), f32),
            vmem((xc, 8, zc), f32),
            vmem((xc + 1, 8, zc), f32),
            vmem((xc + 1, yc + 8, zc), f32),
            vmem((xc, yc, zc), f32),
            vmem((xc, yc, zc), f32),
            vmem((4, 3, xc + 2, yc + 8, zc), f32),
            vmem((4, 3, xc, yc + 8, zc), f32),
            vmem((8, 8, 128), f32),
            vmem((8, 128), f32),
            vmem((peers, 8, 128), f32),
            pltpu.SemaphoreType.DMA((32,)),
            pltpu.SemaphoreType.DMA((32,)),
            pltpu.SemaphoreType.DMA((peers,)),
            pltpu.SemaphoreType.DMA((peers,)),
        ],
        compiler_params=pltpu.CompilerParams(
            collective_id=0, has_side_effects=True, vmem_limit_bytes=60 * 1024 * 1024
        ),
        cost_estimate=pl.CostEstimate(
            flops=600 * xc * yc * zc, bytes_accessed=40 * xc * yc * zc, transcendentals=0
        ),
    )(body_force, phase_label, grain_modulus)


def solution(mesh):
    in_specs = (
        P(None, ("group", "gx"), "gy", None),
        P(("group", "gx"), "gy", None),
        P(("group", "gx"), "gy", None),
    )
    out_specs = (P(None, ("group", "gx"), "gy", None), P(("group", "gx"), "gy", None))
    return jax.shard_map(
        functools.partial(per_device, mesh.shape["gx"]),
        mesh=mesh, in_specs=in_specs, out_specs=out_specs, check_vma=False,
    )
```

```python
import functools
import math

import jax
import jax.numpy as jnp
import numpy as np
from jax import lax
from jax.experimental import pallas as pl
from jax.experimental.pallas import tpu as pltpu
from jax.sharding import PartitionSpec as P

PORE = 0.05
SHIFT = 1.0
MESH = pl.DeviceIdType.MESH


def element_matrix():
    poisson = 0.3
    lame = poisson / ((1.0 + poisson) * (1.0 - 2.0 * poisson))
    shear = 0.5 / (1.0 + poisson)
    elastic = np.zeros((6, 6))
    elastic[:3, :3] = lame
    for index in range(3):
        elastic[index, index] += 2.0 * shear
        elastic[index + 3, index + 3] = shear
    gauss = [0.5 - 0.5 / math.sqrt(3.0), 0.5 + 0.5 / math.sqrt(3.0)]
    matrix = np.zeros((24, 24))
    for px in gauss:
        for py in gauss:
            for pz in gauss:
                strain = np.zeros((6, 24))
                corner = 0
                for sx in (0, 1):
                    for sy in (0, 1):
                        for sz in (0, 1):
                            wx = px if sx else 1.0 - px
                            wy = py if sy else 1.0 - py
                            wz = pz if sz else 1.0 - pz
                            dx = (2 * sx - 1) * wy * wz
                            dy = (2 * sy - 1) * wx * wz
                            dz = (2 * sz - 1) * wx * wy
                            col = 3 * corner
                            strain[0, col] = dx
                            strain[1, col + 1] = dy
                            strain[2, col + 2] = dz
                            strain[3, col] = dy
                            strain[3, col + 1] = dx
                            strain[4, col + 1] = dz
                            strain[4, col + 2] = dy
                            strain[5, col] = dz
                            strain[5, col + 2] = dx
                            corner += 1
                matrix += strain.T @ elastic @ strain / 8.0
    return matrix


def mode_matrix():
    pair = np.array([[1.0, 1.0], [-1.0, 1.0]])
    full = np.kron(np.kron(np.kron(pair, pair), pair), np.eye(3))
    return full @ element_matrix() @ full.T / 64.0


K0_DIAGONAL = float(element_matrix()[0, 0])


def constants():
    k = mode_matrix()
    at = lambda mode, comp: 3 * mode + comp
    return dict(
        normal_own=k[at(4, 0), at(4, 0)] - k[at(4, 0), at(2, 1)],
        normal_all=k[at(4, 0), at(2, 1)],
        shear=k[at(2, 0), at(4, 1)],
        pair_own=k[at(6, 0), at(6, 0)],
        pair_other=k[at(6, 0), at(3, 2)],
        triple=k[at(3, 0), at(5, 1)],
        third=k[at(7, 0), at(7, 0)],
    )


K = {name: float(value) for name, value in constants().items()}


def mode_forces(m, modulus):
    g = {}
    own, every = modulus * K["normal_own"], modulus * K["normal_all"]
    keys = [(4, 0), (2, 1), (1, 2)]
    total = every * (m[keys[0]] + m[keys[1]] + m[keys[2]])
    for key in keys:
        g[key] = own * m[key] + total
    shear = modulus * K["shear"]
    for first, second in (((2, 0), (4, 1)), ((1, 1), (2, 2)), ((1, 0), (4, 2))):
        g[first] = g[second] = shear * (m[first] + m[second])
    own, other = modulus * K["pair_own"], modulus * K["pair_other"]
    for first, second in (((6, 0), (3, 2)), ((6, 1), (5, 2)), ((5, 0), (3, 1))):
        g[first] = own * m[first] + other * m[second]
        g[second] = own * m[second] + other * m[first]
    keys = [(3, 0), (5, 1), (6, 2)]
    triple = modulus * K["triple"]
    total = m[keys[0]] + m[keys[1]] + m[keys[2]]
    for key in keys:
        g[key] = triple * (m[key] + total)
    third = modulus * K["third"]
    for comp in range(3):
        g[(7, comp)] = third * m[(7, comp)]
    return g


def mode_energy(m):
    a, b, c = m[(4, 0)], m[(2, 1)], m[(1, 2)]
    total = a + b + c
    energy = K["normal_own"] * (a * a + b * b + c * c) + K["normal_all"] * (total * total)
    squares = None
    for first, second in (((2, 0), (4, 1)), ((1, 1), (2, 2)), ((1, 0), (4, 2))):
        both = m[first] + m[second]
        squares = both * both if squares is None else squares + both * both
    energy = energy + K["shear"] * squares
    squares = cross = None
    for first, second in (((6, 0), (3, 2)), ((6, 1), (5, 2)), ((5, 0), (3, 1))):
        square = m[first] * m[first] + m[second] * m[second]
        product = m[first] * m[second]
        squares = square if squares is None else squares + square
        cross = product if cross is None else cross + product
    energy = energy + K["pair_own"] * squares + (2.0 * K["pair_other"]) * cross
    a, b, c = m[(3, 0)], m[(5, 1)], m[(6, 2)]
    total = a + b + c
    energy = energy + K["triple"] * (a * a + b * b + c * c + total * total)
    a, b, c = m[(7, 0)], m[(7, 1)], m[(7, 2)]
    return energy + K["third"] * (a * a + b * b + c * c)


def kernel(
    n_gx, xc, yc, zc,
    force_in, label_in, grain_in, disp_out, sens_out,
    force, label, grain, in_sem, final, sens, out_sem,
    u0, u1, u2, edge_out, edge_in, mod_own, mod_halo, mod_edge_out, mod_edge_in,
    mod_ext, diag, inv, yz, out, sums, tile, tiles, send_sem, recv_sem, tile_send, tile_recv,
):
    levels = [u0, u1, u2]
    rows = yc + 8
    base = 8
    gx, gy = lax.axis_index("gx"), lax.axis_index("gy")
    other = 1 - gy
    nxt, prv = lax.rem(gx + 1, n_gx), lax.rem(gx + n_gx - 1, n_gx)
    peers = []
    for step in range(n_gx):
        for flip in (0, 1):
            if step or flip:
                peers.append({
                    "gx": lax.rem(gx + step, n_gx) if step else gx,
                    "gy": other if flip else gy,
                })

    loads = []
    for index, (src, dst) in enumerate(((label_in, label), (grain_in, grain), (force_in, force))):
        load = pltpu.make_async_copy(src, dst, in_sem.at[index])
        load.start()
        loads.append(load)
    barrier = pltpu.get_barrier_semaphore()
    for peer in peers:
        pl.semaphore_signal(barrier, inc=1, device_id=peer, device_id_type=MESH)

    lane = lax.broadcasted_iota(jnp.int32, (1, zc), 1)

    def below(value):
        return jnp.where(lane == 0, 0.0, pltpu.roll(value, 1, 1))

    def above(value):
        return jnp.where(lane == zc - 1, 0.0, pltpu.roll(value, zc - 1, 1))

    sent = []

    def send(src, dst, to_gx, to_gy):
        copy = pltpu.make_async_remote_copy(
            src_ref=src, dst_ref=dst,
            send_sem=send_sem.at[len(sent)], recv_sem=recv_sem.at[len(sent)],
            device_id={"gx": to_gx, "gy": to_gy}, device_id_type=MESH,
        )
        copy.start()
        sent.append(copy)
        return copy

    for x in range(xc + 1):
        mod_ext[x, yc + 1 : rows] = jnp.zeros((rows - yc - 1, zc), jnp.float32)
    for u in levels:
        for c in range(3):
            for x in range(xc + 2):
                u[c, x, base + yc : base + yc + 8] = jnp.zeros((8, zc), jnp.float32)
    for x in range(xc):
        mod_edge_out[x, 1:8] = jnp.zeros((7, zc), jnp.float32)
        for level in range(3):
            edge_out[level, x, 6:8] = jnp.zeros((2, zc), jnp.float32)
    sums[...] = jnp.zeros_like(sums)

    loads[0].wait()
    loads[1].wait()
    for x in range(xc):
        values = jnp.where(label[x] == 1, grain[x], jnp.float32(PORE))
        mod_own[x] = values
        mod_edge_out[x, 0:1] = values[yc - 1 : yc]
        mod_ext[x + 1, 1 : yc + 1] = values
    pl.semaphore_wait(barrier, len(peers))
    mod_y = send(mod_edge_out, mod_edge_in.at[pl.ds(1, xc)], gx, other)
    mod_x = send(mod_own.at[xc - 1], mod_halo, nxt, gy)
    mod_xy = send(mod_edge_out.at[xc - 1], mod_edge_in.at[0], nxt, other)

    def folded(value):
        total = None
        for r in range(value.shape[0] // 8):
            for l in range(zc // 128):
                part = value[8 * r : 8 * r + 8, 128 * l : 128 * l + 128]
                total = part if total is None else total + part
        return total

    def set_edges(level, x, c, value):
        edge_out[level, x - 1, c : c + 1] = value[0:1]
        edge_out[level, x - 1, 3 + c : 4 + c] = value[yc - 1 : yc]

    own = pl.ds(base, yc)

    def send_y(level):
        return send(edge_out.at[level], edge_in.at[level, pl.ds(1, xc)], gx, other)

    def face_next(level, c):
        u = levels[level]
        return send(u.at[c, xc, own], u.at[c, 0, own], nxt, gy)

    def face_prev(level, c):
        u = levels[level]
        return send(u.at[c, 1, own], u.at[c, xc + 1, own], prv, gy)

    def rows_next(level):
        return send(edge_out.at[level, xc - 1], edge_in.at[level, 0], nxt, other)

    def rows_prev(level):
        return send(edge_out.at[level, 0], edge_in.at[level, xc + 1], prv, other)

    def fill_edges(level, x):
        for c in range(3):
            levels[level][c, x, base + yc : base + yc + 1] = edge_in[level, x, c : c + 1]
            levels[level][c, x, base - 1 : base] = edge_in[level, x, 3 + c : 4 + c]

    from_prev, from_next = [[], [], []], [[], [], []]

    def faces(x, level, c):
        if x == xc and level < 2:
            from_prev[level].append(face_next(level, c))
        if x == 1:
            from_next[level].append(face_prev(level, c))

    def start_plane(x, faces):
        total = mod_ext[x - 1, 0:yc] + mod_ext[x - 1, 1 : yc + 1]
        total = total + mod_ext[x, 0:yc] + mod_ext[x, 1 : yc + 1]
        total = (total + above(total)) * K0_DIAGONAL
        inverse = 1.0 / total
        diag[x - 1] = total
        inv[x - 1] = inverse
        for c in range(3):
            load = force[c, x - 1]
            value = inverse * load
            u0[c, x, base : base + yc] = value
            set_edges(0, x, c, value)
            faces(x, 0, c)
            sums[0] += folded(value * load)

    loads[2].wait()
    mod_y.wait_recv()
    for x in range(1, xc + 1):
        mod_ext[x, 0:1] = mod_edge_in[x, 0:1]
    for x in range(xc, 1, -1):
        start_plane(x, faces)
        if x == xc:
            from_prev[0].append(rows_next(0))
    mod_x.wait_recv()
    mod_xy.wait_recv()
    mod_ext[0, 0:1] = mod_edge_in[0, 0:1]
    mod_ext[0, 1 : yc + 1] = mod_halo[...]
    start_plane(1, faces)
    if xc == 1:
        from_prev[0].append(rows_next(0))
    from_next[0].append(rows_prev(0))
    from_y = send_y(0)

    def split_modes(u, x, first, count):
        for c in range(3):
            low = u[c, x, base + first : base + first + count]
            high = u[c, x, base + first + 1 : base + first + 1 + count]
            total, change = high + low, high - low
            low = below(total)
            yz[0, c, x, 0:count] = total + low
            yz[1, c, x, 0:count] = total - low
            low = below(change)
            yz[2, c, x, 0:count] = change + low
            yz[3, c, x, 0:count] = change - low

    def modes_of(cell, r, l):
        m = {}
        for q in range(4):
            for c in range(3):
                low, high = yz[q, c, cell, r, l], yz[q, c, cell + 1, r, l]
                if q:
                    m[(q, c)] = high + low
                m[(4 + q, c)] = high - low
        return m

    lanes = zc // 128

    def apply_cell(cell):
        def body(t, carry):
            r = pl.ds(pl.multiple_of(t // lanes * 8, 8), 8)
            l = pl.ds(pl.multiple_of(lax.rem(t, lanes) * 128, 128), 128)
            g = mode_forces(modes_of(cell, r, l), mod_ext[cell, r, l])
            for q in range(4):
                for c in range(3):
                    if cell >= 1:
                        value = g[(q, c)] - g[(4 + q, c)] if q else -g[(4 + q, c)]
                        if cell == xc:
                            value = value + out[q, c, cell - 1, r, l] if xc > 1 else value
                        elif cell > 1:
                            value = value + out[q, c, cell - 1, r, l]
                        out[q, c, cell - 1, r, l] = value
                    if cell + 1 <= xc:
                        value = g[(q, c)] + g[(4 + q, c)] if q else g[(4 + q, c)]
                        if cell == 0:
                            value = value + out[q, c, cell, r, l]
                        out[q, c, cell, r, l] = value
            return carry

        lax.fori_loop(0, rows // 8 * lanes, body, 0)

    def next_plane(level, x):
        u, v = levels[level], levels[level + 1]
        for c in range(3):
            part = lambda q, start: out[q, c, x - 1, start : start + yc]
            even = (part(0, 0) + part(2, 0)) + (part(0, 1) - part(2, 1))
            odd = (part(1, 0) + part(3, 0)) + (part(1, 1) - part(3, 1))
            image = (even + odd) + above(even - odd)
            value = u[c, x, base : base + yc]
            weighted = image - SHIFT * (diag[x - 1] * value)
            following = inv[x - 1] * weighted
            v[c, x, base : base + yc] = following
            set_edges(level + 1, x, c, following)
            faces(x, level + 1, c)
            sums[2 * level + 1] += folded(value * weighted)
            sums[2 * level + 2] += folded(following * weighted)

    for level in range(2):
        u = levels[level]
        from_y.wait_recv()
        for x in range(1, xc + 1):
            fill_edges(level, x)
            split_modes(u, x, -1, rows)
        for cell in range(1, xc):
            apply_cell(cell)
        for copy in from_next[level]:
            copy.wait_recv()
        fill_edges(level, xc + 1)
        split_modes(u, xc + 1, -1, rows)
        apply_cell(xc)
        for x in range(xc, 1, -1):
            next_plane(level, x)
            if x == xc and level == 0:
                from_prev[1].append(rows_next(1))
        for copy in from_prev[level]:
            copy.wait_recv()
        fill_edges(level, 0)
        split_modes(u, 0, -1, rows)
        apply_cell(0)
        next_plane(level, 1)
        if xc == 1 and level == 0:
            from_prev[1].append(rows_next(1))
        from_next[level + 1].append(rows_prev(level + 1))
        from_y = send_y(level + 1)

    def energies(cell, put):
        def body(t, carry):
            r = pl.ds(pl.multiple_of(t // lanes * 8, 8), 8)
            l = pl.ds(pl.multiple_of(lax.rem(t, lanes) * 128, 128), 128)
            put(r, l, mod_own[cell - 1, r, l] * mode_energy(modes_of(cell, r, l)))
            return carry

        lax.fori_loop(0, yc // 8 * lanes, body, 0)

    def add_energy(r, l, value):
        sums[5] += value

    from_y.wait_recv()
    for x in range(1, xc + 1):
        fill_edges(2, x)
        split_modes(u2, x, 0, yc)
    for cell in range(1, xc):
        energies(cell, add_energy)
    for copy in from_next[2]:
        copy.wait_recv()
    fill_edges(2, xc + 1)
    split_modes(u2, xc + 1, 0, yc)
    energies(xc, add_energy)

    tile[...] = jnp.sum(sums[...], axis=1)
    copies = []
    for index, peer in enumerate(peers):
        copy = pltpu.make_async_remote_copy(
            src_ref=tile, dst_ref=tiles.at[index],
            send_sem=tile_send.at[index], recv_sem=tile_recv.at[index],
            device_id=peer, device_id_type=MESH,
        )
        copy.start()
        copies.append(copy)
    total = tile[...]
    for index, copy in enumerate(copies):
        copy.wait_recv()
        total = total + tiles[index]
    total = jnp.sum(total, axis=1, keepdims=True)
    h = [total[k : k + 1] for k in range(6)]
    h[5] = h[5] - SHIFT * h[4]

    def inner(first, second, shifted):
        result = None
        for i, a in enumerate(first):
            for j, b in enumerate(second):
                moment = h[i + j + 1] + SHIFT * h[i + j] if shifted else h[i + j]
                term = a * b * moment
                result = term if result is None else result + term
        return result

    one = jnp.ones_like(h[0])
    precond, direction = [one], [one]
    weights = [jnp.zeros_like(one)] * 3
    norm_now = h[0]
    for step in range(3):
        alpha = norm_now / inner(direction, direction, True)
        for i, d in enumerate(direction):
            weights[i] = weights[i] + alpha * d
        if step < 2:
            image = [SHIFT * d for d in direction] + [jnp.zeros_like(one)]
            for i, d in enumerate(direction):
                image[i + 1] = image[i + 1] + d
            precond = precond + [jnp.zeros_like(one)] * (len(image) - len(precond))
            precond = [p - alpha * q for p, q in zip(precond, image)]
            norm_next = inner(precond, precond, False)
            beta = norm_next / norm_now
            longer = direction + [jnp.zeros_like(one)]
            direction = [p + beta * d for p, d in zip(precond, longer)]
            norm_now = norm_next

    stores = []
    for x in range(1, xc + 2):
        for c in range(3):
            where = (c, x, slice(base, base + yc + 8))
            value = weights[0] * u0[where] + weights[1] * u1[where] + weights[2] * u2[where]
            final[where] = value
        if x <= xc:
            copy = pltpu.make_async_copy(final.at[:, x, own], disp_out.at[:, x - 1], out_sem.at[x - 1])
            copy.start()
            stores.append(copy)
        split_modes(final, x, 0, yc)

    for cell in range(1, xc + 1):
        def put(r, l, value, cell=cell):
            sens[cell - 1, r, l] = -value

        energies(cell, put)
        copy = pltpu.make_async_copy(sens.at[cell - 1], sens_out.at[cell - 1], out_sem.at[xc + cell - 1])
        copy.start()
        stores.append(copy)

    for copy in sent + copies:
        copy.wait_send()
    for copy in stores:
        copy.wait()


def per_device(n_gx, body_force, phase_label, grain_modulus):
    xc, yc, zc = phase_label.shape
    peers = 2 * n_gx - 1
    f32 = jnp.float32
    vmem = pltpu.VMEM
    ext = vmem((3, xc + 2, yc + 16, zc), f32)
    return pl.pallas_call(
        functools.partial(kernel, n_gx, xc, yc, zc),
        out_shape=(
            jax.ShapeDtypeStruct(body_force.shape, f32),
            jax.ShapeDtypeStruct(phase_label.shape, f32),
        ),
        in_specs=[pl.BlockSpec(memory_space=pl.ANY)] * 3,
        out_specs=(pl.BlockSpec(memory_space=pl.ANY),) * 2,
        scratch_shapes=[
            vmem((3, xc, yc, zc), f32),
            vmem((xc, yc, zc), jnp.int32),
            vmem((xc, yc, zc), f32),
            pltpu.SemaphoreType.DMA((3,)),
            ext,
            vmem((xc, yc, zc), f32),
            pltpu.SemaphoreType.DMA((2 * xc,)),
            ext, ext, ext,
            vmem((3, xc, 8, zc), f32),
            vmem((3, xc + 2, 8, zc), f32),
            vmem((xc, yc, zc), f32),
            vmem((yc, zc), f32),
            vmem((xc, 8, zc), f32),
            vmem((xc + 1, 8, zc), f32),
            vmem((xc + 1, yc + 8, zc), f32),
            vmem((xc, yc, zc), f32),
            vmem((xc, yc, zc), f32),
            vmem((4, 3, xc + 2, yc + 8, zc), f32),
            vmem((4, 3, xc, yc + 8, zc), f32),
            vmem((8, 8, 128), f32),
            vmem((8, 128), f32),
            vmem((peers, 8, 128), f32),
            pltpu.SemaphoreType.DMA((32,)),
            pltpu.SemaphoreType.DMA((32,)),
            pltpu.SemaphoreType.DMA((peers,)),
            pltpu.SemaphoreType.DMA((peers,)),
        ],
        compiler_params=pltpu.CompilerParams(
            collective_id=0, has_side_effects=True, vmem_limit_bytes=60 * 1024 * 1024
        ),
        cost_estimate=pl.CostEstimate(
            flops=600 * xc * yc * zc, bytes_accessed=40 * xc * yc * zc, transcendentals=0
        ),
    )(body_force, phase_label, grain_modulus)


def solution(mesh):
    in_specs = (
        P(None, ("group", "gx"), "gy", None),
        P(("group", "gx"), "gy", None),
        P(("group", "gx"), "gy", None),
    )
    out_specs = (P(None, ("group", "gx"), "gy", None), P(("group", "gx"), "gy", None))
    return jax.shard_map(
        functools.partial(per_device, mesh.shape["gx"]),
        mesh=mesh, in_specs=in_specs, out_specs=out_specs, check_vma=False,
    )
```
